32 devices in a mesh: lon: 2 (over x), lat: 4 (over z), lev: 4 (over y, core).
Axes of the slice: x: 2, y: 2, z: 4, core: 2. Of those that a mesh axis runs over, the one named last changes fastest.
Arguments:
- solution: float32 [36, 8, 32, 256], P(None, 'lev', 'lat', 'lon'), may hold values from -6 to 6
- residual: float32 [36, 8, 32, 256], P(None, 'lev', 'lat', 'lon'), may hold values from -24 to 24
- direction: float32 [36, 8, 32, 256], P(None, 'lev', 'lat', 'lon'), may hold values from -24 to 24
- ensemble: bfloat16 [32, 4, 8, 32, 256], P(None, None, 'lev', 'lat', 'lon'), may hold values from -6 to 6
- static_sd: float32 [4, 8, 32, 256], P(None, 'lev', 'lat', 'lon'), may hold values from 0.5 to 2
- send_tile: int32 [4, 2, 4, 8, 2], P('lev', 'lon', 'lat'), may hold values from 0 to 15
- pair_count: int32 [4, 2, 4, 8], P('lev', 'lon', 'lat'), may hold values from 1 to 2, as said below
- obs_weight: bfloat16 [4, 2, 4, 8, 2, 8, 512], P('lev', 'lon', 'lat'), may hold values from -0.25 to 0.25
- obs_precision: float32 [4, 2, 4, 8, 2, 8], P('lev', 'lon', 'lat'), may hold values from 100 to 3000
Outputs:
- new_solution: float32 [36, 8, 32, 256], P(None, 'lev', 'lat', 'lon')
- new_residual: float32 [36, 8, 32, 256], P(None, 'lev', 'lat', 'lon')
- new_direction: float32 [36, 8, 32, 256], P(None, 'lev', 'lat', 'lon')
The draws below stay inside these ranges and needn't reach their ends.
Inputs may be any that keep to these rules, and one draw needn't show every extreme that they name: `pair_count`: every device sends at least one and at most 2 live slots to every owner of its level plane; in every level plane some owner has 2 live slots from every device of the plane.
All inputs are finite; a program needn't handle non-finite values.
Results may differ from the reference program's by a relative error of at most 0.0034.
Values may be sent and summed in bfloat16 or wider, within the bound.
A program may use at most 64 MiB of HBM per device.

```python
import math
import jax
import jax.numpy as jnp
from jax import lax

MEMBERS = 32
VARS = 4
CLEV = 2
CLAT = 8
CLON = 128
SLOTS = 2
OBS = 8
FIELDS = 36
TILES = 16
GROUP = 8
NLEV = 8
NLAT = 32
NLON = 256
N_LON = 2
N_LAT = 4
N_LEV = 4


def scaled_field(key, reverse):
    key_list = jax.random.split(key, 3)
    field_scale = jnp.exp(jax.random.uniform(key_list[0], (FIELDS, 1, 1, 1), jnp.float32, 0.0, jnp.log(2.0)))
    row_scale = jnp.exp(jax.random.uniform(key_list[1], (1, NLEV, NLAT, 1), jnp.float32, 0.0, jnp.log(2.0)))
    lon_ramp = jnp.arange(NLON, dtype=jnp.float32) / NLON
    if reverse:
        lon_ramp = 1.0 - lon_ramp
    lon_scale = jnp.exp(jnp.log(3.0) * lon_ramp).reshape(1, 1, 1, NLON)
    scale_field = 0.5 * field_scale * row_scale * lon_scale
    noise_field = jnp.clip(jax.random.normal(key_list[2], (FIELDS, NLEV, NLAT, NLON), jnp.float32), -4.0, 4.0)
    return noise_field * scale_field


def draw_residual(key, part):
    return scaled_field(jax.random.fold_in(key, 11), False)


def draw_direction(key, part):
    return scaled_field(jax.random.fold_in(key, 23), True)


def draw_pair_count(key, part):
    key_list = jax.random.split(jax.random.fold_in(key, 37), 3)
    base_count = jax.random.randint(key_list[0], (N_LEV, N_LON, N_LAT, GROUP), 1, SLOTS + 1)
    owner_limit = jax.random.randint(key_list[1], (N_LEV, 1, 1, GROUP), 1, SLOTS + 1)
    base_count = jnp.minimum(base_count, owner_limit)
    busiest = jax.random.randint(key_list[2], (N_LEV, 1, 1, 1), 0, GROUP)
    column = jnp.arange(GROUP, dtype=jnp.int32).reshape(1, 1, 1, GROUP)
    return jnp.where(column == busiest, SLOTS, base_count).astype(jnp.int32)


def plant(drawn, rng, least, largest):
    place = [jax.random.randint(jax.random.fold_in(rng, axis), (), 0, length) for axis, length in enumerate(drawn.shape)]
    widest = drawn.shape.index(max(drawn.shape))
    next_to = place[:widest] + [(place[widest] + 1) % drawn.shape[widest]] + place[widest + 1:]
    return drawn.at[tuple(place)].set(least).at[tuple(next_to)].set(largest)


def steps_of(key, shape, pieces, low, top_value):
    loudness, own = 1.0, jax.random.fold_in(key, 6)
    for position, parts in pieces:
        heights = jnp.exp(jax.random.uniform(jax.random.fold_in(own, position), (parts,), jnp.float32, low / len(pieces), top_value / len(pieces)))
        loudness = loudness * jnp.repeat(heights, shape[position] // parts).reshape([-1 if axis == position else 1 for axis in range(len(shape))])
    return loudness


def bell_draw(own_key, dims, width, reach, pieces=(), held_as=jnp.bfloat16):
    values = width * jax.random.normal(own_key, dims, jnp.float32)
    if pieces:
        values = values * steps_of(own_key, dims, pieces, -0.22, 0.18)
    return jnp.clip(values, -reach, reach).astype(held_as)


def setup_inputs(seed: int = 0) -> dict:
    keys = jax.random.split(jax.random.key(seed), 10)
    solution = bell_draw(keys[0], (FIELDS, NLEV, NLAT, NLON), 1.0, 6.0, ((1, 4), (2, 4), (3, 2)), jnp.float32)
    residual = draw_residual(jax.random.fold_in(keys[9], 71), 0)
    direction = draw_direction(jax.random.fold_in(keys[9], 71), 0)
    ensemble = bell_draw(keys[3], (MEMBERS, VARS, NLEV, NLAT, NLON), 1.0, 6.0, ((2, 4), (3, 4), (4, 2)))
    static_sd = jnp.clip(jnp.exp(math.log(2.0) - 1.3862944 * jax.random.uniform(keys[4], (VARS, NLEV, NLAT, NLON), jnp.float32) ** steps_of(keys[4], (VARS, NLEV, NLAT, NLON), ((1, 4), (2, 4), (3, 2)), -0.2, 0.2)), 0.5, 2.0)
    send_tile = plant(jax.random.randint(keys[5], (N_LEV, N_LON, N_LAT, GROUP, SLOTS), 0, TILES), jax.random.fold_in(keys[5], 1), 0, TILES - 1).astype(jnp.int32)
    pair_count = draw_pair_count(jax.random.fold_in(keys[9], 71), 0)
    obs_weight = bell_draw(keys[7], (N_LEV, N_LON, N_LAT, GROUP, SLOTS, OBS, VARS * CLON), (VARS * CLON) ** -0.5, 0.25, ((0, 4), (1, 2), (2, 4)))
    obs_precision = jnp.clip(jnp.exp(math.log(3000.0) - 3.4011974 * jax.random.uniform(keys[8], (N_LEV, N_LON, N_LAT, GROUP, SLOTS, OBS), jnp.float32) ** steps_of(keys[8], (N_LEV, N_LON, N_LAT, GROUP, SLOTS, OBS), ((0, 4), (1, 2), (2, 4)), -0.2, 0.2)), 100.0, 3000.0)
    return dict(solution=solution, residual=residual, direction=direction, ensemble=ensemble, static_sd=static_sd, send_tile=send_tile, pair_count=pair_count, obs_weight=obs_weight, obs_precision=obs_precision)


spread_lon = 0.075
spread_lat = 0.3
spread_lev = 0.075
ens_share = 0.75
static_part = 0.5


def one_pass(padded):
    centre = padded[:, 1:-1, 1:-1, 1:-1]
    result = centre * (1.0 - 2.0 * (spread_lon + spread_lat + spread_lev))
    result = result + spread_lon * (padded[:, 1:-1, 1:-1, 2:] + padded[:, 1:-1, 1:-1, :-2])
    result = result + spread_lat * (padded[:, 1:-1, 2:, 1:-1] + padded[:, 1:-1, :-2, 1:-1])
    result = result + spread_lev * (padded[:, 2:, 1:-1, 1:-1] + padded[:, :-2, 1:-1, 1:-1])
    return result


def smooth(fields):
    for pass_index in range(4):
        wrapped = jnp.concatenate([fields[:, :, :, -1:], fields, fields[:, :, :, :1]], axis=3)
        padded = jnp.pad(wrapped, ((0, 0), (1, 1), (1, 1), (0, 0)))
        fields = one_pass(padded)
    return fields


def owner_work(operands):
    weights, arrived, precision = operands
    weights_wide = weights.astype(jnp.float32)
    predicted = jnp.einsum("gsbc,gsc->gsb", weights_wide, arrived.astype(jnp.float32))
    weighted = (precision * predicted).astype(jnp.bfloat16)
    return jnp.einsum("gsbc,gsb->gsc", weights_wide, weighted.astype(jnp.float32))


def reference(solution, residual, direction, ensemble, static_sd, send_tile, pair_count, obs_weight, obs_precision):
    scale_ens = (ens_share / MEMBERS) ** 0.5
    tile_width = VARS * CLON
    start_norm = jnp.sum(residual * residual)
    smoothed = smooth(direction)
    ens_part = jnp.sum(ensemble.astype(jnp.float32) * smoothed[:MEMBERS, None], axis=0)
    increment = (scale_ens * ens_part + static_part * static_sd * smoothed[MEMBERS:]).astype(jnp.bfloat16)
    blocks = increment.reshape(VARS, N_LEV, CLEV, N_LAT, CLAT, N_LON, CLON)
    tile_table = blocks.transpose(1, 5, 3, 2, 4, 0, 6).reshape(N_LEV, N_LON, N_LAT, TILES, tile_width)
    tile_pick = send_tile.reshape(N_LEV, N_LON, N_LAT, GROUP * SLOTS).astype(jnp.int32)
    outgoing = jnp.take_along_axis(tile_table, tile_pick[:, :, :, :, None], axis=3)
    is_live = jnp.arange(SLOTS, dtype=jnp.int32)[None, None, None, None, :] < pair_count[:, :, :, :, None]
    is_live = is_live.reshape(N_LEV, N_LON, N_LAT, GROUP * SLOTS)
    outgoing = jnp.where(is_live[:, :, :, :, None], outgoing, jnp.zeros_like(outgoing))
    outgoing = outgoing.reshape(N_LEV, GROUP, GROUP, SLOTS, tile_width)
    arrived = jnp.swapaxes(outgoing, 1, 2).reshape(N_LEV * GROUP, GROUP, SLOTS, tile_width)
    weights = obs_weight.reshape(N_LEV * GROUP, GROUP, SLOTS, OBS, tile_width)
    precision = obs_precision.reshape(N_LEV * GROUP, GROUP, SLOTS, OBS)
    returned = lax.map(owner_work, (weights, arrived, precision))
    returned = jnp.swapaxes(returned.reshape(N_LEV, GROUP, GROUP, SLOTS, tile_width), 1, 2)
    returned = returned.reshape(N_LEV, N_LON, N_LAT, GROUP * SLOTS, tile_width)
    one_hot = (tile_pick[:, :, :, :, None] == jnp.arange(TILES, dtype=jnp.int32)).astype(jnp.float32)
    adj_tiles = jnp.einsum("lopt,lopc->lotc", one_hot.reshape(N_LEV, GROUP, GROUP * SLOTS, TILES), returned.reshape(N_LEV, GROUP, GROUP * SLOTS, tile_width), precision=lax.Precision.HIGHEST)
    adj_tiles = adj_tiles.reshape(N_LEV, N_LON, N_LAT, CLEV, CLAT, VARS, CLON)
    adjoint = adj_tiles.transpose(5, 0, 3, 2, 4, 1, 6).reshape(VARS, NLEV, NLAT, NLON)
    back_ens = scale_ens * jnp.sum(ensemble.astype(jnp.float32) * adjoint[None], axis=1)
    back_static = static_part * static_sd * adjoint
    back = jnp.concatenate([back_ens, back_static], axis=0)
    image_field = direction + smooth(back)
    curvature = jnp.sum(direction * image_field)
    step_size = start_norm / curvature
    new_solution = solution + step_size * direction
    new_residual = residual - step_size * image_field
    next_norm = jnp.sum(new_residual * new_residual)
    new_direction = new_residual + (next_norm / (start_norm + 1e-6)) * direction
    return new_solution, new_residual, new_direction
```

```python
import functools

import jax
import jax.numpy as jnp
from jax import lax
from jax.experimental import pallas as pl
from jax.experimental.pallas import tpu as pltpu
from jax.sharding import PartitionSpec as P

spread_lon = 0.075
spread_lat = 0.3
spread_lev = 0.075
ens_share = 0.75
static_part = 0.5
centre_share = 1.0 - 2.0 * (spread_lon + spread_lat + spread_lev)
PASSES = 4
AXES = ("lon", "lat", "lev")
MESH = pl.DeviceIdType.MESH
f32 = jnp.float32
bf16 = jnp.bfloat16


def each(count, step):
    if count <= 32:
        for k in range(count):
            step(k)
    else:
        lax.fori_loop(0, count, lambda k, carry: (step(k), carry)[1], 0)


def kernel(
    sizes,
    direction,
    residual,
    ensemble,
    static_sd,
    obs_weight,
    obs_precision,
    send_tile,
    pair_count,
    image_out,
    scalars_out,
    field_a,
    field_b,
    lev_send,
    lev_recv,
    lat_send,
    lat_recv,
    lon_send,
    lon_recv,
    tiles_out,
    tiles_in,
    ret_out,
    ret_in,
    sum_send,
    sum_plane,
    sum_lev,
    halo_ssem,
    halo_rsem,
    a2a_ssem,
    a2a_rsem,
    plane_ssem,
    plane_rsem,
    col_ssem,
    col_rsem,
):
    n_lon, n_lat, n_lev = sizes
    members, variables, levels, rows, lanes = ensemble.shape
    fields = direction.shape[0]
    blocks = fields * levels
    group = n_lon * n_lat
    slots = send_tile.shape[4]
    tiles = levels * rows
    scale_ens = (ens_share / members) ** 0.5
    at_lon, at_lat, at_lev = (lax.axis_index(a) for a in AXES)
    me = at_lon * n_lat + at_lat

    def plane_id(k):
        peer = lax.rem(me + k, group)
        return peer, {"lon": peer // n_lat, "lat": lax.rem(peer, n_lat)}

    def lev_id(k):
        return {"lev": lax.rem(at_lev + k, n_lev)}

    barrier = pltpu.get_barrier_semaphore()

    def greet_plane(k):
        pl.semaphore_signal(barrier, inc=1, device_id=plane_id(k + 1)[1], device_id_type=MESH)

    def greet_lev(k):
        pl.semaphore_signal(barrier, inc=1, device_id=lev_id(k + 1), device_id_type=MESH)

    each(group - 1, greet_plane)
    each(n_lev - 1, greet_lev)

    buffers = {"lev": (lev_send, lev_recv), "lat": (lat_send, lat_recv), "lon": (lon_send, lon_recv)}
    places = {"lev": (at_lev, n_lev), "lat": (at_lat, n_lat), "lon": (at_lon, n_lon)}

    def halo_copy(p, axis, side):
        src, dst = buffers[axis]
        place, count = places[axis]
        number = AXES.index(axis)
        return pltpu.make_async_remote_copy(
            src_ref=src.at[p, side],
            dst_ref=dst.at[p, 1 - side],
            send_sem=halo_ssem.at[p, number, side],
            recv_sem=halo_rsem.at[p, number, 1 - side],
            device_id={axis: lax.rem(place + (count - 1 if side == 0 else 1), count)},
            device_id_type=MESH,
        )

    def if_there(axis, side, act):
        place, count = places[axis]
        if axis == "lon":
            act()
        else:
            pl.when(place > 0 if side == 0 else place < count - 1)(act)

    lane_of = lax.broadcasted_iota(jnp.int32, (1, rows, lanes), 2)
    row_of = lax.broadcasted_iota(jnp.int32, (1, rows, lanes), 1)
    west = jnp.where(lane_of > 0, spread_lon, 0.0)
    east = jnp.where(lane_of < lanes - 1, spread_lon, 0.0)
    south = jnp.where(row_of > 0, spread_lat, 0.0)
    north = jnp.where(row_of < rows - 1, spread_lat, 0.0)
    edge_row = lax.broadcasted_iota(jnp.int32, (8, lanes), 0)
    edge_lane = lax.broadcasted_iota(jnp.int32, (8, lanes), 1)
    edges = ((edge_row == 0) & (edge_lane == 0)) | ((edge_row == 1) & (edge_lane == lanes - 1))
    edges = edges.astype(bf16)
    lat_pad = lat_send.shape[2] - blocks

    def send_halos(p, src):
        x4 = src[...].reshape(fields, levels, rows, lanes)
        for side, level in ((0, 0), (1, levels - 1)):
            lev_send[p, side] = x4[:, level].reshape(fields * rows, lanes).astype(bf16)
            if_there("lev", side, lambda side=side: halo_copy(p, "lev", side).start())
        for side, row in ((0, 0), (1, rows - 1)):
            edge = src[pl.ds(row, blocks, stride=rows), :]
            if lat_pad:
                edge = jnp.concatenate([edge, jnp.zeros((lat_pad, lanes), f32)], axis=0)
            lat_send[p, side] = edge.astype(bf16)
            if_there("lat", side, lambda side=side: halo_copy(p, "lat", side).start())
        packed = lax.dot_general(
            edges, src[...].astype(bf16), (((1,), (1,)), ((), ())), preferred_element_type=f32
        )
        for side in (0, 1):
            lon_send[p, side] = packed[side : side + 1]
            halo_copy(p, "lon", side).start()

    chunk = max(c for c in range(1, 13) if fields % c == 0)

    def local_part(src, dst):
        for first in range(0, fields, chunk):
            span = pl.ds(first * levels * rows, chunk * levels * rows)
            x = src[span, :].reshape(chunk * levels, rows, lanes)
            y = x * centre_share
            y = y + west * pltpu.roll(x, 1, 2) + east * pltpu.roll(x, lanes - 1, 2)
            y = y + south * pltpu.roll(x, 1, 1) + north * pltpu.roll(x, rows - 1, 1)
            x4 = x.reshape(chunk, levels, rows, lanes)
            if levels > 1:
                none = jnp.zeros((chunk, 1, rows, lanes), f32)
                above = jnp.concatenate([x4[:, 1:], none], axis=1)
                below = jnp.concatenate([none, x4[:, :-1]], axis=1)
                y = y + spread_lev * (above + below).reshape(chunk * levels, rows, lanes)
            dst[span, :] = y.reshape(chunk * levels * rows, lanes)

    def add_halos(p, dst):
        for side in (0, 1):
            halo_copy(p, "lon", 1 - side).wait_recv()
        ends = jnp.concatenate(
            [lon_recv[p, 0], lon_recv[p, 1], jnp.zeros((6, blocks * rows), f32)], axis=0
        )
        spill = lax.dot_general(
            ends.astype(bf16), edges, (((0,), (0,)), ((), ())), preferred_element_type=f32
        )
        dst[...] += spread_lon * spill
        for side, row in ((0, 0), (1, rows - 1)):
            if_there("lat", side, lambda side=side: halo_copy(p, "lat", 1 - side).wait_recv())
            edge = lat_recv[p, side].astype(f32)[:blocks]
            at = pl.ds(row, blocks, stride=rows)
            dst[at, :] = dst[at, :] + spread_lat * edge
        for side in (0, 1):
            if_there("lev", side, lambda side=side: halo_copy(p, "lev", 1 - side).wait_recv())
        low = lev_recv[p, 0].astype(f32).reshape(fields, 1, rows, lanes) * spread_lev
        high = lev_recv[p, 1].astype(f32).reshape(fields, 1, rows, lanes) * spread_lev
        y4 = dst[...].reshape(fields, levels, rows, lanes)
        if levels == 1:
            y4 = y4 + low + high
        else:
            inner = [y4[:, 1:-1]] if levels > 2 else []
            y4 = jnp.concatenate([y4[:, :1] + low, *inner, y4[:, -1:] + high], axis=1)
        dst[...] = y4.reshape(blocks * rows, lanes)

    def smooth(first_pass):
        src, dst = field_a, field_b
        for p in range(first_pass, first_pass + PASSES):
            send_halos(p, src)
            local_part(src, dst)
            add_halos(p, dst)
            src, dst = dst, src
        return src

    field_a[...] = direction[...].reshape(blocks * rows, lanes)
    for side in (0, 1):
        for axis in ("lat", "lev"):
            place, count = places[axis]

            def clear(axis=axis, side=side):
                for p in range(2 * PASSES):
                    ref = buffers[axis][1]
                    ref[p, side] = jnp.zeros(ref.shape[2:], ref.dtype)

            pl.when(place == 0 if side == 0 else place == count - 1)(clear)

    total = slots * group

    def slot_code(i):
        s, d = i // group, i % group
        tile = send_tile[0, 0, 0, d, s]
        return jnp.where(s < pair_count[0, 0, 0, d], tile, -1)

    def fill(dim, shape):
        where_at = lax.broadcasted_iota(jnp.int32, shape, dim)
        step = lambda i, codes: jnp.where(where_at == i, slot_code(i), codes)
        codes = jnp.zeros(shape, jnp.int32)
        if total <= 32:
            for i in range(total):
                codes = step(i, codes)
        else:
            codes = lax.fori_loop(0, total, step, codes)
        return (codes == lax.broadcasted_iota(jnp.int32, shape, 1 - dim)).astype(f32)

    pick = fill(0, (total, tiles)).astype(bf16)
    place_back = fill(1, (tiles, total))

    obs = obs_precision.shape[5]
    eye = (
        lax.broadcasted_iota(jnp.int32, (1, obs, obs), 1)
        == lax.broadcasted_iota(jnp.int32, (1, obs, obs), 2)
    ).astype(f32)
    precision = [
        jnp.sum(obs_precision[0, 0, 0][:, s : s + 1, :] * eye, axis=2, keepdims=True)
        for s in range(slots)
    ]
    d_all = direction[...]
    r_all = residual[...]
    direction_norm = jnp.sum(d_all * d_all)
    residual_norm = jnp.sum(r_all * r_all)

    pl.semaphore_wait(barrier, group - 1 + n_lev - 1)

    smoothed = smooth(0)

    sm4 = smoothed[...].reshape(fields, levels, rows, lanes)
    ens_part = jnp.zeros((variables, levels, rows, lanes), f32)
    for k in range(members):
        ens_part = ens_part + ensemble[k].astype(f32) * sm4[k][None]
    increment = scale_ens * ens_part + static_part * static_sd[...] * sm4[members:]
    increment = increment.astype(bf16).reshape(variables, tiles, lanes)
    table = jnp.concatenate([increment[v] for v in range(variables)], axis=1)
    outgoing = jnp.dot(pick, table, preferred_element_type=f32)
    height = slots * variables
    for s in range(slots):
        for v in range(variables):
            part = outgoing[s * group : (s + 1) * group, v * lanes : (v + 1) * lanes]
            tiles_out[pl.ds(s * variables + v, group, stride=height), :] = part

    def block_of(ref, g):
        return ref.at[pl.ds(pl.multiple_of(g * height, height), height), :]

    def exchange(turn, src, dst):
        def copy(k):
            peer, device = plane_id(k + 1)
            return pltpu.make_async_remote_copy(
                src_ref=block_of(src, peer),
                dst_ref=block_of(dst, me),
                send_sem=a2a_ssem.at[turn, k],
                recv_sem=a2a_rsem.at[turn, k],
                device_id=device,
                device_id_type=MESH,
            )

        return copy

    def own_block(src, dst):
        block_of(dst, me)[...] = block_of(src, me)[...]

    there = exchange(0, tiles_out, tiles_in)
    each(group - 1, lambda k: there(k).start())
    own_block(tiles_out, tiles_in)
    each(group - 1, lambda k: there(k).wait_recv())

    arrived = tiles_in[...].reshape(group, height, lanes)
    fit = jnp.zeros((1, 1), f32)
    for s in range(slots):
        weights = [
            obs_weight[0, 0, 0, :, s, :, v * lanes : (v + 1) * lanes].astype(f32)
            for v in range(variables)
        ]
        product = jnp.zeros((group, obs, lanes), f32)
        for v in range(variables):
            at = s * variables + v
            product = product + weights[v] * arrived[:, at : at + 1, :]
        predicted = jnp.sum(product, axis=2, keepdims=True)
        weighted = (precision[s] * predicted).astype(bf16).astype(f32)
        fit = fit + jnp.sum(jnp.sum(predicted * weighted, axis=0), axis=0, keepdims=True)
        for v in range(variables):
            ret = jnp.sum(weights[v] * weighted, axis=1, keepdims=True)
            ret_out[pl.ds(s * variables + v, group, stride=height), :] = ret.reshape(group, lanes)

    back_again = exchange(1, ret_out, ret_in)
    each(group - 1, lambda k: back_again(k).start())
    own_block(ret_out, ret_in)

    def sum_copies(turn):
        def plane(k):
            return pltpu.make_async_remote_copy(
                src_ref=sum_send.at[turn, 0],
                dst_ref=sum_plane.at[turn, k + 1],
                send_sem=plane_ssem.at[turn, k],
                recv_sem=plane_rsem.at[turn, k],
                device_id=plane_id(k + 1)[1],
                device_id_type=MESH,
            )

        def column(k):
            return pltpu.make_async_remote_copy(
                src_ref=sum_send.at[turn, 1],
                dst_ref=sum_lev.at[turn, k + 1],
                send_sem=col_ssem.at[turn, k],
                recv_sem=col_rsem.at[turn, k],
                device_id=lev_id(k + 1),
                device_id_type=MESH,
            )

        return plane, column

    def sum_begin(turn, values):
        plane, column = sum_copies(turn)
        sum_send[turn, 0] = values
        sum_plane[turn, 0] = values
        each(group - 1, lambda k: plane(k).start())

    def sum_middle(turn):
        plane, column = sum_copies(turn)
        each(group - 1, lambda k: plane(k).wait_recv())
        values = jnp.sum(sum_plane[turn], axis=0)
        sum_send[turn, 1] = values
        sum_lev[turn, 0] = values
        each(n_lev - 1, lambda k: column(k).start())

    def sum_end(turn):
        plane, column = sum_copies(turn)
        each(n_lev - 1, lambda k: column(k).wait_recv())
        return jnp.sum(sum_lev[turn], axis=0)

    row8 = lax.broadcasted_iota(jnp.int32, (8, lanes), 0)
    mine = jnp.where(row8 == 0, residual_norm, jnp.where(row8 == 1, direction_norm, 0.0))
    sum_begin(0, mine + jnp.where(row8 == 2, fit, 0.0))

    each(group - 1, lambda k: back_again(k).wait_recv())
    came = jnp.concatenate(
        [
            jnp.concatenate(
                [
                    ret_in[pl.ds(s * variables + v, group, stride=height), :]
                    for v in range(variables)
                ],
                axis=1,
            )
            for s in range(slots)
        ],
        axis=0,
    )
    adjoint = jnp.dot(
        place_back, came, precision=lax.Precision.HIGHEST, preferred_element_type=f32
    )
    adjoint = jnp.stack(
        [
            adjoint[:, v * lanes : (v + 1) * lanes].reshape(levels, rows, lanes)
            for v in range(variables)
        ]
    )
    scaled = scale_ens * adjoint
    deep = levels * rows
    for k in range(members):
        value = jnp.sum(ensemble[k].astype(f32) * scaled, axis=0)
        field_a[k * deep : (k + 1) * deep, :] = value.reshape(deep, lanes)
    still = static_part * static_sd[...] * adjoint
    field_a[members * deep :, :] = still.reshape(variables * deep, lanes)
    sum_middle(0)

    smooth_back = smooth(PASSES)

    totals = sum_end(0)
    start_norm = totals[0:1]
    step = start_norm / (totals[1:2] + totals[2:3])
    image = direction[...] + smooth_back[...].reshape(fields, levels, rows, lanes)
    image_out[...] = image
    left = residual[...] - step * image
    next_norm = jnp.sum(left * left)
    sum_begin(1, jnp.full((8, lanes), next_norm, f32))
    sum_middle(1)
    totals = sum_end(1)
    ratio = totals / (start_norm + 1e-6)
    scalars_out[...] = jnp.where(row8 == 0, step, ratio)

    for p in range(2 * PASSES):
        for axis in AXES:
            for side in (0, 1):
                if_there(axis, side, lambda: halo_copy(p, axis, side).wait_send())
    for copy in (there, back_again):
        each(group - 1, lambda k: copy(k).wait_send())
    for turn in (0, 1):
        plane, column = sum_copies(turn)
        each(group - 1, lambda k: plane(k).wait_send())
        each(n_lev - 1, lambda k: column(k).wait_send())


def body(
    sizes,
    solution,
    residual,
    direction,
    ensemble,
    static_sd,
    send_tile,
    pair_count,
    obs_weight,
    obs_precision,
):
    n_lon, n_lat, n_lev = sizes
    members, variables, levels, rows, lanes = ensemble.shape
    fields = direction.shape[0]
    blocks = fields * levels
    group = n_lon * n_lat
    slots = send_tile.shape[4]
    height = slots * variables
    passes = 2 * PASSES
    lat_rows = -(-blocks // 16) * 16
    vmem = pl.BlockSpec(memory_space=pltpu.VMEM)
    smem = pl.BlockSpec(memory_space=pltpu.SMEM)
    dma = pltpu.SemaphoreType.DMA
    image, scalars = pl.pallas_call(
        functools.partial(kernel, sizes),
        out_shape=[
            jax.ShapeDtypeStruct(direction.shape, f32),
            jax.ShapeDtypeStruct((8, lanes), f32),
        ],
        in_specs=[vmem] * 6 + [smem] * 2,
        out_specs=[vmem] * 2,
        scratch_shapes=[
            pltpu.VMEM((blocks * rows, lanes), f32),
            pltpu.VMEM((blocks * rows, lanes), f32),
            pltpu.VMEM((passes, 2, fields * rows, lanes), bf16),
            pltpu.VMEM((passes, 2, fields * rows, lanes), bf16),
            pltpu.VMEM((passes, 2, lat_rows, lanes), bf16),
            pltpu.VMEM((passes, 2, lat_rows, lanes), bf16),
            pltpu.VMEM((passes, 2, 1, blocks * rows), f32),
            pltpu.VMEM((passes, 2, 1, blocks * rows), f32),
            pltpu.VMEM((group * height, lanes), f32),
            pltpu.VMEM((group * height, lanes), f32),
            pltpu.VMEM((group * height, lanes), f32),
            pltpu.VMEM((group * height, lanes), f32),
            pltpu.VMEM((2, 2, 8, lanes), f32),
            pltpu.VMEM((2, group, 8, lanes), f32),
            pltpu.VMEM((2, n_lev, 8, lanes), f32),
            dma((passes, 3, 2)),
            dma((passes, 3, 2)),
            dma((2, group)),
            dma((2, group)),
            dma((2, group)),
            dma((2, group)),
            dma((2, n_lev)),
            dma((2, n_lev)),
        ],
        compiler_params=pltpu.CompilerParams(
            collective_id=0, has_side_effects=True, vmem_limit_bytes=40 * 1024 * 1024
        ),
        cost_estimate=pl.CostEstimate(flops=10**8, bytes_accessed=3 * 10**6, transcendentals=0),
        name="cg_step",
    )(
        direction,
        residual,
        ensemble,
        static_sd,
        obs_weight,
        obs_precision,
        send_tile,
        pair_count,
    )
    step = scalars[0, 0]
    ratio = scalars[1, 0]
    new_residual = residual - step * image
    return (
        solution + step * direction,
        new_residual,
        new_residual + ratio * direction,
    )


def solution(mesh):
    sizes = tuple(mesh.shape[axis] for axis in AXES)
    field = P(None, "lev", "lat", "lon")
    in_specs = (
        field,
        field,
        field,
        P(None, None, "lev", "lat", "lon"),
        field,
        P("lev", "lon", "lat", None, None),
        P("lev", "lon", "lat", None),
        P("lev", "lon", "lat", None, None, None, None),
        P("lev", "lon", "lat", None, None, None),
    )
    return jax.shard_map(
        functools.partial(body, sizes),
        mesh=mesh,
        in_specs=in_specs,
        out_specs=(field, field, field),
        check_vma=False,
    )
```

```python
import functools

import jax
import jax.numpy as jnp
from jax import lax
from jax.experimental import pallas as pl
from jax.experimental.pallas import tpu as pltpu
from jax.sharding import PartitionSpec as P

spread_lon = 0.075
spread_lat = 0.3
spread_lev = 0.075
ens_share = 0.75
static_part = 0.5
centre_share = 1.0 - 2.0 * (spread_lon + spread_lat + spread_lev)
PASSES = 4
PARTS = 2
AXES = ("lon", "lat", "lev")
MESH = pl.DeviceIdType.MESH
f32 = jnp.float32
bf16 = jnp.bfloat16


def each(count, step):
    if count <= 32:
        for k in range(count):
            step(k)
    else:
        lax.fori_loop(0, count, lambda k, carry: (step(k), carry)[1], 0)


def kernel(
    sizes,
    direction_hbm,
    residual_hbm,
    ensemble_hbm,
    static_sd_hbm,
    obs_weight_hbm,
    obs_precision_hbm,
    send_tile,
    pair_count,
    image_out,
    step_out,
    ratio_out,
    direction,
    residual,
    ensemble,
    static_sd,
    obs_weight,
    obs_precision,
    fetch_sem,
    field_a,
    field_b,
    lev_send,
    lev_recv,
    lat_send,
    lat_recv,
    lon_send,
    lon_recv,
    tiles_out,
    tiles_in,
    ret_out,
    ret_in,
    sum_send,
    sum_plane,
    sum_lev,
    halo_ssem,
    halo_rsem,
    a2a_ssem,
    a2a_rsem,
    plane_ssem,
    plane_rsem,
    col_ssem,
    col_rsem,
):
    n_lon, n_lat, n_lev = sizes
    members, variables, levels, rows, lanes = ensemble.shape
    fields = direction.shape[0]
    blocks = fields * levels
    group = n_lon * n_lat
    slots = send_tile.shape[3]
    tiles = levels * rows
    scale_ens = (ens_share / members) ** 0.5
    at_lon, at_lat, at_lev = (lax.axis_index(a) for a in AXES)
    held = (direction, residual, ensemble, static_sd, obs_weight, obs_precision)
    origins = (
        direction_hbm,
        residual_hbm,
        ensemble_hbm,
        static_sd_hbm,
        obs_weight_hbm,
        obs_precision_hbm,
    )
    fetches = [
        pltpu.make_async_copy(src, dst, fetch_sem.at[i])
        for i, (src, dst) in enumerate(zip(origins, held))
    ]
    for fetch in fetches:
        fetch.start()
    me = at_lon * n_lat + at_lat

    def plane_id(k):
        peer = lax.rem(me + k, group)
        return peer, {"lon": peer // n_lat, "lat": lax.rem(peer, n_lat)}

    def lev_id(k):
        return {"lev": lax.rem(at_lev + k, n_lev)}

    barrier = pltpu.get_barrier_semaphore()

    def greet_plane(k):
        pl.semaphore_signal(barrier, inc=1, device_id=plane_id(k + 1)[1], device_id_type=MESH)

    def greet_lev(k):
        pl.semaphore_signal(barrier, inc=1, device_id=lev_id(k + 1), device_id_type=MESH)

    each(group - 1, greet_plane)
    each(n_lev - 1, greet_lev)

    buffers = {"lev": (lev_send, lev_recv), "lat": (lat_send, lat_recv), "lon": (lon_send, lon_recv)}
    places = {"lev": (at_lev, n_lev), "lat": (at_lat, n_lat), "lon": (at_lon, n_lon)}

    def halo_copy(p, h, axis, side):
        src, dst = buffers[axis]
        place, count = places[axis]
        number = AXES.index(axis)
        return pltpu.make_async_remote_copy(
            src_ref=src.at[p, h, side],
            dst_ref=dst.at[p, h, 1 - side],
            send_sem=halo_ssem.at[p, h, number, side],
            recv_sem=halo_rsem.at[p, h, number, 1 - side],
            device_id={axis: lax.rem(place + (count - 1 if side == 0 else 1), count)},
            device_id_type=MESH,
        )

    def if_there(axis, side, act):
        place, count = places[axis]
        if axis == "lon":
            act()
        else:
            pl.when(place > 0 if side == 0 else place < count - 1)(act)

    lane_of = lax.broadcasted_iota(jnp.int32, (1, rows, lanes), 2)
    row_of = lax.broadcasted_iota(jnp.int32, (1, rows, lanes), 1)
    west = jnp.where(lane_of > 0, spread_lon, 0.0)
    east = jnp.where(lane_of < lanes - 1, spread_lon, 0.0)
    south = jnp.where(row_of > 0, spread_lat, 0.0)
    north = jnp.where(row_of < rows - 1, spread_lat, 0.0)
    edge_row = lax.broadcasted_iota(jnp.int32, (8, lanes), 0)
    edge_lane = lax.broadcasted_iota(jnp.int32, (8, lanes), 1)
    edges = ((edge_row == 0) & (edge_lane == 0)) | ((edge_row == 1) & (edge_lane == lanes - 1))
    edges = edges.astype(bf16)
    part_fields = fields // PARTS
    part_blocks = part_fields * levels
    part_rows = part_blocks * rows
    lat_pad = lat_send.shape[3] - part_blocks

    def send_halos(p, h, src):
        start = h * part_rows
        x = src[start : start + part_rows, :]
        x4 = x.reshape(part_fields, levels, rows, lanes)
        for side, level in ((0, 0), (1, levels - 1)):
            lev_send[p, h, side] = x4[:, level].reshape(part_fields * rows, lanes).astype(bf16)
            if_there("lev", side, lambda side=side: halo_copy(p, h, "lev", side).start())
        packed = lax.dot_general(
            edges, x.astype(bf16), (((1,), (1,)), ((), ())), preferred_element_type=f32
        )
        for side, row in ((0, 0), (1, rows - 1)):
            edge = src[pl.ds(start + row, part_blocks, stride=rows), :]
            if lat_pad:
                edge = jnp.concatenate([edge, jnp.zeros((lat_pad, lanes), f32)], axis=0)
            lat_send[p, h, side] = edge.astype(bf16)
            if_there("lat", side, lambda side=side: halo_copy(p, h, "lat", side).start())
        for side in (0, 1):
            lon_send[p, h, side] = packed[side : side + 1]
            halo_copy(p, h, "lon", side).start()

    chunk = max(c for c in range(1, 10) if part_fields % c == 0)

    def local_part(h, src, dst):
        for first in range(0, part_fields, chunk):
            span = pl.ds(h * part_rows + first * levels * rows, chunk * levels * rows)
            x = src[span, :].reshape(chunk * levels, rows, lanes)
            y = x * centre_share
            y = y + west * pltpu.roll(x, 1, 2) + east * pltpu.roll(x, lanes - 1, 2)
            y = y + south * pltpu.roll(x, 1, 1) + north * pltpu.roll(x, rows - 1, 1)
            x4 = x.reshape(chunk, levels, rows, lanes)
            if levels > 1:
                none = jnp.zeros((chunk, 1, rows, lanes), f32)
                above = jnp.concatenate([x4[:, 1:], none], axis=1)
                below = jnp.concatenate([none, x4[:, :-1]], axis=1)
                y = y + spread_lev * (above + below).reshape(chunk * levels, rows, lanes)
            dst[span, :] = y.reshape(chunk * levels * rows, lanes)

    def add_halos(p, h, dst):
        start = h * part_rows
        for side in (0, 1):
            halo_copy(p, h, "lon", 1 - side).wait_recv()
        ends = jnp.concatenate(
            [lon_recv[p, h, 0], lon_recv[p, h, 1], jnp.zeros((6, part_rows), f32)], axis=0
        )
        spill = lax.dot_general(
            ends.astype(bf16), edges, (((0,), (0,)), ((), ())), preferred_element_type=f32
        )
        for side, row in ((0, 0), (1, rows - 1)):
            if_there("lat", side, lambda side=side: halo_copy(p, h, "lat", 1 - side).wait_recv())
            edge = lat_recv[p, h, side].astype(f32)[:part_blocks]
            at = pl.ds(start + row, part_blocks, stride=rows)
            dst[at, :] = dst[at, :] + spread_lat * edge
        for side in (0, 1):
            if_there("lev", side, lambda side=side: halo_copy(p, h, "lev", 1 - side).wait_recv())
        low = lev_recv[p, h, 0].astype(f32).reshape(part_fields, 1, rows, lanes) * spread_lev
        high = lev_recv[p, h, 1].astype(f32).reshape(part_fields, 1, rows, lanes) * spread_lev
        y = dst[start : start + part_rows, :] + spread_lon * spill
        y4 = y.reshape(part_fields, levels, rows, lanes)
        if levels == 1:
            y4 = y4 + low + high
        else:
            inner = [y4[:, 1:-1]] if levels > 2 else []
            y4 = jnp.concatenate([y4[:, :1] + low, *inner, y4[:, -1:] + high], axis=1)
        dst[start : start + part_rows, :] = y4.reshape(part_rows, lanes)

    def smooth(first_pass, meanwhile):
        src, dst = field_a, field_b
        for p in range(first_pass, first_pass + PASSES):
            for h in range(PARTS):
                if p == first_pass and h == 0:
                    meanwhile()
                local_part(h, src, dst)
                add_halos(p, h, dst)
                if p < first_pass + PASSES - 1:
                    send_halos(p + 1, h, dst)
            src, dst = dst, src
        return src

    for side in (0, 1):
        for axis in ("lat", "lev"):
            place, count = places[axis]

            def clear(axis=axis, side=side):
                ref = buffers[axis][1]
                for p in range(2 * PASSES):
                    for h in range(PARTS):
                        ref[p, h, side] = jnp.zeros(ref.shape[3:], ref.dtype)

            pl.when(place == 0 if side == 0 else place == count - 1)(clear)

    total = slots * group

    def slot_code(i):
        s, d = i // group, i % group
        tile = send_tile[0, 0, 0, s, d]
        return jnp.where(s < pair_count[0, 0, 0, d], tile, -1)

    def fill(dim, shape):
        where_at = lax.broadcasted_iota(jnp.int32, shape, dim)
        step = lambda i, codes: jnp.where(where_at == i, slot_code(i), codes)
        codes = jnp.zeros(shape, jnp.int32)
        if total <= 32:
            for i in range(total):
                codes = step(i, codes)
        else:
            codes = lax.fori_loop(0, total, step, codes)
        return (codes == lax.broadcasted_iota(jnp.int32, shape, 1 - dim)).astype(f32)

    pick = fill(0, (total, tiles)).astype(bf16)
    place_back = fill(1, (tiles, total))

    obs = obs_precision.shape[5]
    eye = (
        lax.broadcasted_iota(jnp.int32, (1, obs, obs), 1)
        == lax.broadcasted_iota(jnp.int32, (1, obs, obs), 2)
    ).astype(f32)
    fetches[0].wait()
    field_a[...] = direction[...].reshape(blocks * rows, lanes)
    pl.semaphore_wait(barrier, group - 1 + n_lev - 1)
    for h in range(PARTS):
        send_halos(0, h, field_a)

    known = []

    def local_sums():
        for fetch in fetches[1:]:
            fetch.wait()
        for s in range(slots):
            row = obs_precision[0, 0, 0][:, s : s + 1, :]
            known.append(jnp.sum(row * eye, axis=2, keepdims=True))
        d_all = direction[...]
        r_all = residual[...]
        known.append(jnp.sum(d_all * d_all))
        known.append(jnp.sum(r_all * r_all))

    smoothed = smooth(0, local_sums)
    precision, direction_norm, residual_norm = known[:slots], known[slots], known[slots + 1]

    sm4 = smoothed[...].reshape(fields, levels, rows, lanes)
    ens_part = jnp.zeros((variables, levels, rows, lanes), f32)
    for k in range(members):
        ens_part = ens_part + ensemble[k].astype(f32) * sm4[k][None]
    increment = scale_ens * ens_part + static_part * static_sd[...] * sm4[members:]
    increment = increment.astype(bf16).reshape(variables, tiles, lanes)
    table = jnp.concatenate([increment[v] for v in range(variables)], axis=1)
    outgoing = jnp.dot(pick, table, preferred_element_type=f32)
    height = slots * variables
    for s in range(slots):
        for v in range(variables):
            part = outgoing[s * group : (s + 1) * group, v * lanes : (v + 1) * lanes]
            tiles_out[pl.ds(s * variables + v, group, stride=height), :] = part

    def block_of(ref, g):
        return ref.at[pl.ds(pl.multiple_of(g * height, height), height), :]

    def exchange(turn, src, dst):
        def copy(k):
            peer, device = plane_id(k + 1)
            return pltpu.make_async_remote_copy(
                src_ref=block_of(src, peer),
                dst_ref=block_of(dst, me),
                send_sem=a2a_ssem.at[turn, k],
                recv_sem=a2a_rsem.at[turn, k],
                device_id=device,
                device_id_type=MESH,
            )

        return copy

    def own_block(src, dst):
        block_of(dst, me)[...] = block_of(src, me)[...]

    there = exchange(0, tiles_out, tiles_in)
    each(group - 1, lambda k: there(k).start())
    own_block(tiles_out, tiles_in)
    each(group - 1, lambda k: there(k).wait_recv())

    arrived = tiles_in[...].reshape(group, height, lanes)
    fit = jnp.zeros((1, 1), f32)
    for s in range(slots):
        weights = [
            obs_weight[0, 0, 0, :, s, :, v * lanes : (v + 1) * lanes].astype(f32)
            for v in range(variables)
        ]
        product = jnp.zeros((group, obs, lanes), f32)
        for v in range(variables):
            at = s * variables + v
            product = product + weights[v] * arrived[:, at : at + 1, :]
        predicted = jnp.sum(product, axis=2, keepdims=True)
        weighted = (precision[s] * predicted).astype(bf16).astype(f32)
        fit = fit + jnp.sum(jnp.sum(predicted * weighted, axis=0), axis=0, keepdims=True)
        for v in range(variables):
            ret = jnp.sum(weights[v] * weighted, axis=1, keepdims=True)
            ret_out[pl.ds(s * variables + v, group, stride=height), :] = ret.reshape(group, lanes)

    back_again = exchange(1, ret_out, ret_in)
    each(group - 1, lambda k: back_again(k).start())
    own_block(ret_out, ret_in)

    def sum_copies(turn):
        def plane(k):
            return pltpu.make_async_remote_copy(
                src_ref=sum_send.at[turn, 0],
                dst_ref=sum_plane.at[turn, k + 1],
                send_sem=plane_ssem.at[turn, k],
                recv_sem=plane_rsem.at[turn, k],
                device_id=plane_id(k + 1)[1],
                device_id_type=MESH,
            )

        def column(k):
            return pltpu.make_async_remote_copy(
                src_ref=sum_send.at[turn, 1],
                dst_ref=sum_lev.at[turn, k + 1],
                send_sem=col_ssem.at[turn, k],
                recv_sem=col_rsem.at[turn, k],
                device_id=lev_id(k + 1),
                device_id_type=MESH,
            )

        return plane, column

    def sum_begin(turn, values):
        plane, column = sum_copies(turn)
        sum_send[turn, 0] = values
        sum_plane[turn, 0] = values
        each(group - 1, lambda k: plane(k).start())

    def sum_middle(turn):
        plane, column = sum_copies(turn)
        each(group - 1, lambda k: plane(k).wait_recv())
        values = jnp.sum(sum_plane[turn], axis=0)
        sum_send[turn, 1] = values
        sum_lev[turn, 0] = values
        each(n_lev - 1, lambda k: column(k).start())

    def sum_end(turn):
        plane, column = sum_copies(turn)
        each(n_lev - 1, lambda k: column(k).wait_recv())
        return jnp.sum(sum_lev[turn], axis=0)

    row8 = lax.broadcasted_iota(jnp.int32, (8, lanes), 0)
    mine = jnp.where(row8 == 0, residual_norm, jnp.where(row8 == 1, direction_norm, 0.0))
    sum_begin(0, mine + jnp.where(row8 == 2, fit, 0.0))

    each(group - 1, lambda k: back_again(k).wait_recv())
    came = jnp.concatenate(
        [
            jnp.concatenate(
                [
                    ret_in[pl.ds(s * variables + v, group, stride=height), :]
                    for v in range(variables)
                ],
                axis=1,
            )
            for s in range(slots)
        ],
        axis=0,
    )
    adjoint = jnp.dot(
        place_back, came, precision=lax.Precision.HIGHEST, preferred_element_type=f32
    )
    adjoint = jnp.stack(
        [
            adjoint[:, v * lanes : (v + 1) * lanes].reshape(levels, rows, lanes)
            for v in range(variables)
        ]
    )
    scaled = scale_ens * adjoint
    deep = levels * rows
    def tell(k):
        if (k + 1) % part_fields == 0:
            send_halos(PASSES, (k + 1) // part_fields - 1, field_a)

    for k in range(members):
        value = jnp.sum(ensemble[k].astype(f32) * scaled, axis=0)
        field_a[k * deep : (k + 1) * deep, :] = value.reshape(deep, lanes)
        tell(k)
    still = static_part * static_sd[...] * adjoint
    field_a[members * deep :, :] = still.reshape(variables * deep, lanes)
    send_halos(PASSES, PARTS - 1, field_a)

    smooth_back = smooth(PASSES, lambda: sum_middle(0))

    totals = sum_end(0)
    start_norm = totals[0:1]
    step = start_norm / (totals[1:2] + totals[2:3])
    image = direction[...] + smooth_back[...].reshape(fields, levels, rows, lanes)
    image_out[...] = image
    left = residual[...] - step * image
    next_norm = jnp.sum(left * left)
    sum_begin(1, jnp.full((8, lanes), next_norm, f32))
    sum_middle(1)
    totals = sum_end(1)
    ratio = totals / (start_norm + 1e-6)
    step_out[...] = jnp.broadcast_to(step, (8, lanes))
    ratio_out[...] = ratio

    for p in range(2 * PASSES):
        for h in range(PARTS):
            for axis in AXES:
                for side in (0, 1):
                    if_there(axis, side, lambda: halo_copy(p, h, axis, side).wait_send())
    for copy in (there, back_again):
        each(group - 1, lambda k: copy(k).wait_send())
    for turn in (0, 1):
        plane, column = sum_copies(turn)
        each(group - 1, lambda k: plane(k).wait_send())
        each(n_lev - 1, lambda k: column(k).wait_send())


def body(
    sizes,
    solution,
    residual,
    direction,
    ensemble,
    static_sd,
    send_tile,
    pair_count,
    obs_weight,
    obs_precision,
):
    n_lon, n_lat, n_lev = sizes
    members, variables, levels, rows, lanes = ensemble.shape
    fields = direction.shape[0]
    blocks = fields * levels
    group = n_lon * n_lat
    slots = send_tile.shape[4]
    height = slots * variables
    passes = 2 * PASSES
    part = fields // PARTS
    lat_rows = -(-(part * levels) // 16) * 16
    vmem = pl.BlockSpec(memory_space=pltpu.VMEM)
    smem = pl.BlockSpec(memory_space=pltpu.SMEM)
    dma = pltpu.SemaphoreType.DMA
    image, step, ratio = pl.pallas_call(
        functools.partial(kernel, sizes),
        out_shape=[
            jax.ShapeDtypeStruct(direction.shape, f32),
            jax.ShapeDtypeStruct((8, lanes), f32),
            jax.ShapeDtypeStruct((8, lanes), f32),
        ],
        in_specs=[pl.BlockSpec(memory_space=pl.ANY)] * 6 + [smem] * 2,
        out_specs=[vmem] * 3,
        scratch_shapes=[
            pltpu.VMEM(direction.shape, f32),
            pltpu.VMEM(residual.shape, f32),
            pltpu.VMEM(ensemble.shape, bf16),
            pltpu.VMEM(static_sd.shape, f32),
            pltpu.VMEM(obs_weight.shape, bf16),
            pltpu.VMEM(obs_precision.shape, f32),
            dma((6,)),
            pltpu.VMEM((blocks * rows, lanes), f32),
            pltpu.VMEM((blocks * rows, lanes), f32),
            pltpu.VMEM((passes, PARTS, 2, part * rows, lanes), bf16),
            pltpu.VMEM((passes, PARTS, 2, part * rows, lanes), bf16),
            pltpu.VMEM((passes, PARTS, 2, lat_rows, lanes), bf16),
            pltpu.VMEM((passes, PARTS, 2, lat_rows, lanes), bf16),
            pltpu.VMEM((passes, PARTS, 2, 1, part * levels * rows), f32),
            pltpu.VMEM((passes, PARTS, 2, 1, part * levels * rows), f32),
            pltpu.VMEM((group * height, lanes), f32),
            pltpu.VMEM((group * height, lanes), f32),
            pltpu.VMEM((group * height, lanes), f32),
            pltpu.VMEM((group * height, lanes), f32),
            pltpu.VMEM((2, 2, 8, lanes), f32),
            pltpu.VMEM((2, group, 8, lanes), f32),
            pltpu.VMEM((2, n_lev, 8, lanes), f32),
            dma((passes, PARTS, 3, 2)),
            dma((passes, PARTS, 3, 2)),
            dma((2, group)),
            dma((2, group)),
            dma((2, group)),
            dma((2, group)),
            dma((2, n_lev)),
            dma((2, n_lev)),
        ],
        compiler_params=pltpu.CompilerParams(
            collective_id=0, has_side_effects=True, vmem_limit_bytes=56 * 1024 * 1024
        ),
        cost_estimate=pl.CostEstimate(flops=10**8, bytes_accessed=3 * 10**6, transcendentals=0),
        name="cg_step",
    )(
        direction,
        residual,
        ensemble,
        static_sd,
        obs_weight,
        obs_precision,
        jnp.swapaxes(send_tile, 3, 4),
        pair_count,
    )
    new_residual = residual - step * image
    return (
        solution + step * direction,
        new_residual,
        new_residual + ratio * direction,
    )


def solution(mesh):
    sizes = tuple(mesh.shape[axis] for axis in AXES)
    field = P(None, "lev", "lat", "lon")
    in_specs = (
        field,
        field,
        field,
        P(None, None, "lev", "lat", "lon"),
        field,
        P("lev", "lon", "lat", None, None),
        P("lev", "lon", "lat", None),
        P("lev", "lon", "lat", None, None, None, None),
        P("lev", "lon", "lat", None, None, None),
    )
    return jax.shard_map(
        functools.partial(body, sizes),
        mesh=mesh,
        in_specs=in_specs,
        out_specs=(field, field, field),
        check_vma=False,
    )
```

```python
import functools

import jax
import jax.numpy as jnp
from jax import lax
from jax.experimental import pallas as pl
from jax.experimental.pallas import tpu as pltpu
from jax.sharding import PartitionSpec as P

spread_lon = 0.075
spread_lat = 0.3
spread_lev = 0.075
ens_share = 0.75
static_part = 0.5
centre_share = 1.0 - 2.0 * (spread_lon + spread_lat + spread_lev)
PASSES = 4
PARTS = 2
AXES = ("lon", "lat", "lev")
MESH = pl.DeviceIdType.MESH
f32 = jnp.float32
bf16 = jnp.bfloat16


def each(count, step):
    if count <= 32:
        for k in range(count):
            step(k)
    else:
        lax.fori_loop(0, count, lambda k, carry: (step(k), carry)[1], 0)


def kernel(
    sizes,
    direction_hbm,
    residual_hbm,
    ensemble_hbm,
    static_sd_hbm,
    obs_weight_hbm,
    obs_precision_hbm,
    send_tile,
    pair_count,
    image_out,
    step_out,
    ratio_out,
    direction,
    residual,
    ensemble,
    static_sd,
    obs_weight,
    obs_precision,
    fetch_sem,
    field_a,
    field_b,
    lev_send,
    lev_recv,
    lat_send,
    lat_recv,
    lon_send,
    lon_recv,
    tiles_out,
    tiles_in,
    ret_out,
    ret_in,
    sum_send,
    sum_plane,
    sum_lev,
    halo_ssem,
    halo_rsem,
    a2a_ssem,
    a2a_rsem,
    plane_ssem,
    plane_rsem,
    col_ssem,
    col_rsem,
):
    n_lon, n_lat, n_lev = sizes
    members, variables, levels, rows, lanes = ensemble.shape
    fields = direction.shape[0]
    blocks = fields * levels
    group = n_lon * n_lat
    slots = send_tile.shape[3]
    tiles = levels * rows
    scale_ens = (ens_share / members) ** 0.5
    at_lon, at_lat, at_lev = (lax.axis_index(a) for a in AXES)
    held = (direction, residual, ensemble, static_sd, obs_weight, obs_precision)
    origins = (
        direction_hbm,
        residual_hbm,
        ensemble_hbm,
        static_sd_hbm,
        obs_weight_hbm,
        obs_precision_hbm,
    )
    fetches = [
        pltpu.make_async_copy(src, dst, fetch_sem.at[i])
        for i, (src, dst) in enumerate(zip(origins, held))
    ]
    for fetch in fetches:
        fetch.start()
    me = at_lon * n_lat + at_lat

    def plane_id(k):
        peer = lax.rem(me + k, group)
        return peer, {"lon": peer // n_lat, "lat": lax.rem(peer, n_lat)}

    def lev_id(k):
        return {"lev": lax.rem(at_lev + k, n_lev)}

    barrier = pltpu.get_barrier_semaphore()

    def greet_plane(k):
        pl.semaphore_signal(barrier, inc=1, device_id=plane_id(k + 1)[1], device_id_type=MESH)

    def greet_lev(k):
        pl.semaphore_signal(barrier, inc=1, device_id=lev_id(k + 1), device_id_type=MESH)

    each(group - 1, greet_plane)
    each(n_lev - 1, greet_lev)

    buffers = {"lev": (lev_send, lev_recv), "lat": (lat_send, lat_recv), "lon": (lon_send, lon_recv)}
    places = {"lev": (at_lev, n_lev), "lat": (at_lat, n_lat), "lon": (at_lon, n_lon)}

    beside = {
        axis: [lax.rem(place + count - 1, count), lax.rem(place + 1, count)]
        for axis, (place, count) in places.items()
    }

    def halo_copy(p, h, axis, side):
        src, dst = buffers[axis]
        number = AXES.index(axis)
        return pltpu.make_async_remote_copy(
            src_ref=src.at[p, h, side],
            dst_ref=dst.at[p, h, 1 - side],
            send_sem=halo_ssem.at[p, h, number, side],
            recv_sem=halo_rsem.at[p, h, number, 1 - side],
            device_id={axis: beside[axis][side]},
            device_id_type=MESH,
        )

    def if_there(axis, side, act):
        place, count = places[axis]
        if axis == "lon":
            act()
        else:
            pl.when(place > 0 if side == 0 else place < count - 1)(act)

    lane_of = lax.broadcasted_iota(jnp.int32, (1, rows, lanes), 2)
    row_of = lax.broadcasted_iota(jnp.int32, (1, rows, lanes), 1)
    west = jnp.where(lane_of > 0, spread_lon, 0.0)
    east = jnp.where(lane_of < lanes - 1, spread_lon, 0.0)
    south = jnp.where(row_of > 0, spread_lat, 0.0)
    north = jnp.where(row_of < rows - 1, spread_lat, 0.0)
    edge_row = lax.broadcasted_iota(jnp.int32, (8, lanes), 0)
    edge_lane = lax.broadcasted_iota(jnp.int32, (8, lanes), 1)
    edges = ((edge_row == 0) & (edge_lane == 0)) | ((edge_row == 1) & (edge_lane == lanes - 1))
    edges = edges.astype(bf16)
    part_fields = fields // PARTS
    part_blocks = part_fields * levels
    part_rows = part_blocks * rows
    lat_pad = lat_send.shape[3] - part_blocks

    def send_halos(p, h, src):
        start = h * part_rows
        x = src[start : start + part_rows, :]
        packed = lax.dot_general(
            edges, x.astype(bf16), (((1,), (1,)), ((), ())), preferred_element_type=f32
        )
        x4 = x.reshape(part_fields, levels, rows, lanes)
        for side, level in ((0, 0), (1, levels - 1)):
            lev_send[p, h, side] = x4[:, level].reshape(part_fields * rows, lanes).astype(bf16)
        for side, row in ((0, 0), (1, rows - 1)):
            edge = src[pl.ds(start + row, part_blocks, stride=rows), :]
            if lat_pad:
                edge = jnp.concatenate([edge, jnp.zeros((lat_pad, lanes), f32)], axis=0)
            lat_send[p, h, side] = edge.astype(bf16)
        for side in (0, 1):
            lon_send[p, h, side] = packed[side : side + 1]
        for side in (0, 1):
            if_there("lev", side, lambda: halo_copy(p, h, "lev", side).start())
        for side in (0, 1):
            if_there("lat", side, lambda: halo_copy(p, h, "lat", side).start())
        for side in (0, 1):
            halo_copy(p, h, "lon", side).start()

    chunk = max(c for c in range(1, 10) if part_fields % c == 0)

    def local_part(h, src, dst):
        for first in range(0, part_fields, chunk):
            span = pl.ds(h * part_rows + first * levels * rows, chunk * levels * rows)
            x = src[span, :].reshape(chunk * levels, rows, lanes)
            y = x * centre_share
            y = y + west * pltpu.roll(x, 1, 2) + east * pltpu.roll(x, lanes - 1, 2)
            y = y + south * pltpu.roll(x, 1, 1) + north * pltpu.roll(x, rows - 1, 1)
            x4 = x.reshape(chunk, levels, rows, lanes)
            if levels > 1:
                none = jnp.zeros((chunk, 1, rows, lanes), f32)
                above = jnp.concatenate([x4[:, 1:], none], axis=1)
                below = jnp.concatenate([none, x4[:, :-1]], axis=1)
                y = y + spread_lev * (above + below).reshape(chunk * levels, rows, lanes)
            dst[span, :] = y.reshape(chunk * levels * rows, lanes)

    def add_halos(p, h, dst):
        start = h * part_rows
        for axis in AXES:
            for side in (0, 1):
                if_there(axis, side, lambda: halo_copy(p, h, axis, 1 - side).wait_recv())
        ends = jnp.concatenate(
            [lon_recv[p, h, 0], lon_recv[p, h, 1], jnp.zeros((6, part_rows), f32)], axis=0
        )
        spill = lax.dot_general(
            ends.astype(bf16), edges, (((0,), (0,)), ((), ())), preferred_element_type=f32
        )
        for side, row in ((0, 0), (1, rows - 1)):
            edge = lat_recv[p, h, side].astype(f32)[:part_blocks]
            at = pl.ds(start + row, part_blocks, stride=rows)
            dst[at, :] = dst[at, :] + spread_lat * edge
        low = lev_recv[p, h, 0].astype(f32).reshape(part_fields, 1, rows, lanes) * spread_lev
        high = lev_recv[p, h, 1].astype(f32).reshape(part_fields, 1, rows, lanes) * spread_lev
        y = dst[start : start + part_rows, :] + spread_lon * spill
        y4 = y.reshape(part_fields, levels, rows, lanes)
        if levels == 1:
            y4 = y4 + low + high
        else:
            inner = [y4[:, 1:-1]] if levels > 2 else []
            y4 = jnp.concatenate([y4[:, :1] + low, *inner, y4[:, -1:] + high], axis=1)
        dst[start : start + part_rows, :] = y4.reshape(part_rows, lanes)

    def smooth(first_pass, meanwhile):
        src, dst = field_a, field_b
        for p in range(first_pass, first_pass + PASSES):
            for h in range(PARTS):
                if p == first_pass and h == 0:
                    meanwhile()
                local_part(h, src, dst)
                add_halos(p, h, dst)
                if p < first_pass + PASSES - 1:
                    send_halos(p + 1, h, dst)
            src, dst = dst, src
        return src

    for side in (0, 1):
        for axis in ("lat", "lev"):
            place, count = places[axis]

            def clear(axis=axis, side=side):
                ref = buffers[axis][1]
                for p in range(2 * PASSES):
                    for h in range(PARTS):
                        ref[p, h, side] = jnp.zeros(ref.shape[3:], ref.dtype)

            pl.when(place == 0 if side == 0 else place == count - 1)(clear)

    total = slots * group

    def slot_code(i):
        s, d = i // group, i % group
        tile = send_tile[0, 0, 0, s, d]
        return jnp.where(s < pair_count[0, 0, 0, d], tile, -1)

    def fill(dim, shape):
        where_at = lax.broadcasted_iota(jnp.int32, shape, dim)
        step = lambda i, codes: jnp.where(where_at == i, slot_code(i), codes)
        codes = jnp.zeros(shape, jnp.int32)
        if total <= 32:
            for i in range(total):
                codes = step(i, codes)
        else:
            codes = lax.fori_loop(0, total, step, codes)
        return (codes == lax.broadcasted_iota(jnp.int32, shape, 1 - dim)).astype(f32)

    pick = fill(0, (total, tiles)).astype(bf16)
    place_back = fill(1, (tiles, total))

    obs = obs_precision.shape[5]
    eye = (
        lax.broadcasted_iota(jnp.int32, (1, obs, obs), 1)
        == lax.broadcasted_iota(jnp.int32, (1, obs, obs), 2)
    ).astype(f32)
    fetches[0].wait()
    field_a[...] = direction[...].reshape(blocks * rows, lanes)
    pl.semaphore_wait(barrier, group - 1 + n_lev - 1)
    for h in range(PARTS):
        send_halos(0, h, field_a)

    known = []

    def local_sums():
        for fetch in fetches[1:]:
            fetch.wait()
        for s in range(slots):
            row = obs_precision[0, 0, 0][:, s : s + 1, :]
            known.append(jnp.sum(row * eye, axis=2, keepdims=True))
        d_all = direction[...]
        r_all = residual[...]
        known.append(jnp.sum(d_all * d_all))
        known.append(jnp.sum(r_all * r_all))

    smoothed = smooth(0, local_sums)
    precision, direction_norm, residual_norm = known[:slots], known[slots], known[slots + 1]

    sm4 = smoothed[...].reshape(fields, levels, rows, lanes)
    ens_part = jnp.zeros((variables, levels, rows, lanes), f32)
    for k in range(members):
        ens_part = ens_part + ensemble[k].astype(f32) * sm4[k][None]
    increment = scale_ens * ens_part + static_part * static_sd[...] * sm4[members:]
    increment = increment.astype(bf16).reshape(variables, tiles, lanes)
    table = jnp.concatenate([increment[v] for v in range(variables)], axis=1)
    outgoing = jnp.dot(pick, table, preferred_element_type=f32)
    height = slots * variables
    for s in range(slots):
        for v in range(variables):
            part = outgoing[s * group : (s + 1) * group, v * lanes : (v + 1) * lanes]
            tiles_out[pl.ds(s * variables + v, group, stride=height), :] = part

    def block_of(ref, g):
        return ref.at[pl.ds(pl.multiple_of(g * height, height), height), :]

    def exchange(turn, src, dst):
        def copy(k):
            peer, device = plane_id(k + 1)
            return pltpu.make_async_remote_copy(
                src_ref=block_of(src, peer),
                dst_ref=block_of(dst, me),
                send_sem=a2a_ssem.at[turn, k],
                recv_sem=a2a_rsem.at[turn, k],
                device_id=device,
                device_id_type=MESH,
            )

        return copy

    def own_block(src, dst):
        block_of(dst, me)[...] = block_of(src, me)[...]

    there = exchange(0, tiles_out, tiles_in)
    each(group - 1, lambda k: there(k).start())
    own_block(tiles_out, tiles_in)
    each(group - 1, lambda k: there(k).wait_recv())

    arrived = tiles_in[...].reshape(group, height, lanes)
    fit = jnp.zeros((1, 1), f32)
    for s in range(slots):
        weights = [
            obs_weight[0, 0, 0, :, s, :, v * lanes : (v + 1) * lanes].astype(f32)
            for v in range(variables)
        ]
        product = jnp.zeros((group, obs, lanes), f32)
        for v in range(variables):
            at = s * variables + v
            product = product + weights[v] * arrived[:, at : at + 1, :]
        predicted = jnp.sum(product, axis=2, keepdims=True)
        weighted = (precision[s] * predicted).astype(bf16).astype(f32)
        fit = fit + jnp.sum(jnp.sum(predicted * weighted, axis=0), axis=0, keepdims=True)
        for v in range(variables):
            ret = jnp.sum(weights[v] * weighted, axis=1, keepdims=True)
            ret_out[pl.ds(s * variables + v, group, stride=height), :] = ret.reshape(group, lanes)

    back_again = exchange(1, ret_out, ret_in)
    each(group - 1, lambda k: back_again(k).start())
    own_block(ret_out, ret_in)

    def sum_copies(turn):
        def plane(k):
            return pltpu.make_async_remote_copy(
                src_ref=sum_send.at[turn, 0],
                dst_ref=sum_plane.at[turn, k + 1],
                send_sem=plane_ssem.at[turn, k],
                recv_sem=plane_rsem.at[turn, k],
                device_id=plane_id(k + 1)[1],
                device_id_type=MESH,
            )

        def column(k):
            return pltpu.make_async_remote_copy(
                src_ref=sum_send.at[turn, 1],
                dst_ref=sum_lev.at[turn, k + 1],
                send_sem=col_ssem.at[turn, k],
                recv_sem=col_rsem.at[turn, k],
                device_id=lev_id(k + 1),
                device_id_type=MESH,
            )

        return plane, column

    def sum_begin(turn, values):
        plane, column = sum_copies(turn)
        sum_send[turn, 0] = values
        sum_plane[turn, 0] = values
        each(group - 1, lambda k: plane(k).start())

    def sum_middle(turn):
        plane, column = sum_copies(turn)
        each(group - 1, lambda k: plane(k).wait_recv())
        values = jnp.sum(sum_plane[turn], axis=0)
        sum_send[turn, 1] = values
        sum_lev[turn, 0] = values
        each(n_lev - 1, lambda k: column(k).start())

    def sum_end(turn):
        plane, column = sum_copies(turn)
        each(n_lev - 1, lambda k: column(k).wait_recv())
        return jnp.sum(sum_lev[turn], axis=0)

    row8 = lax.broadcasted_iota(jnp.int32, (8, lanes), 0)
    mine = jnp.where(row8 == 0, residual_norm, jnp.where(row8 == 1, direction_norm, 0.0))
    sum_begin(0, mine + jnp.where(row8 == 2, fit, 0.0))

    each(group - 1, lambda k: back_again(k).wait_recv())
    came = jnp.concatenate(
        [
            jnp.concatenate(
                [
                    ret_in[pl.ds(s * variables + v, group, stride=height), :]
                    for v in range(variables)
                ],
                axis=1,
            )
            for s in range(slots)
        ],
        axis=0,
    )
    adjoint = jnp.dot(
        place_back, came, precision=lax.Precision.HIGHEST, preferred_element_type=f32
    )
    adjoint = jnp.stack(
        [
            adjoint[:, v * lanes : (v + 1) * lanes].reshape(levels, rows, lanes)
            for v in range(variables)
        ]
    )
    scaled = scale_ens * adjoint
    deep = levels * rows
    def tell(k):
        if (k + 1) % part_fields == 0:
            send_halos(PASSES, (k + 1) // part_fields - 1, field_a)

    for k in range(members):
        value = jnp.sum(ensemble[k].astype(f32) * scaled, axis=0)
        field_a[k * deep : (k + 1) * deep, :] = value.reshape(deep, lanes)
        tell(k)
    still = static_part * static_sd[...] * adjoint
    field_a[members * deep :, :] = still.reshape(variables * deep, lanes)
    send_halos(PASSES, PARTS - 1, field_a)

    smooth_back = smooth(PASSES, lambda: sum_middle(0))

    totals = sum_end(0)
    start_norm = totals[0:1]
    step = start_norm / (totals[1:2] + totals[2:3])
    image = direction[...] + smooth_back[...].reshape(fields, levels, rows, lanes)
    image_out[...] = image
    left = residual[...] - step * image
    next_norm = jnp.sum(left * left)
    sum_begin(1, jnp.full((8, lanes), next_norm, f32))
    sum_middle(1)
    totals = sum_end(1)
    ratio = totals / (start_norm + 1e-6)
    step_out[...] = jnp.broadcast_to(step, (8, lanes))
    ratio_out[...] = ratio

    for p in range(2 * PASSES):
        for h in range(PARTS):
            for axis in AXES:
                for side in (0, 1):
                    if_there(axis, side, lambda: halo_copy(p, h, axis, side).wait_send())
    for copy in (there, back_again):
        each(group - 1, lambda k: copy(k).wait_send())
    for turn in (0, 1):
        plane, column = sum_copies(turn)
        each(group - 1, lambda k: plane(k).wait_send())
        each(n_lev - 1, lambda k: column(k).wait_send())


def body(
    sizes,
    solution,
    residual,
    direction,
    ensemble,
    static_sd,
    send_tile,
    pair_count,
    obs_weight,
    obs_precision,
):
    n_lon, n_lat, n_lev = sizes
    members, variables, levels, rows, lanes = ensemble.shape
    fields = direction.shape[0]
    blocks = fields * levels
    group = n_lon * n_lat
    slots = send_tile.shape[4]
    height = slots * variables
    passes = 2 * PASSES
    part = fields // PARTS
    lat_rows = -(-(part * levels) // 16) * 16
    vmem = pl.BlockSpec(memory_space=pltpu.VMEM)
    smem = pl.BlockSpec(memory_space=pltpu.SMEM)
    dma = pltpu.SemaphoreType.DMA
    image, step, ratio = pl.pallas_call(
        functools.partial(kernel, sizes),
        out_shape=[
            jax.ShapeDtypeStruct(direction.shape, f32),
            jax.ShapeDtypeStruct((8, lanes), f32),
            jax.ShapeDtypeStruct((8, lanes), f32),
        ],
        in_specs=[pl.BlockSpec(memory_space=pl.ANY)] * 6 + [smem] * 2,
        out_specs=[vmem] * 3,
        scratch_shapes=[
            pltpu.VMEM(direction.shape, f32),
            pltpu.VMEM(residual.shape, f32),
            pltpu.VMEM(ensemble.shape, bf16),
            pltpu.VMEM(static_sd.shape, f32),
            pltpu.VMEM(obs_weight.shape, bf16),
            pltpu.VMEM(obs_precision.shape, f32),
            dma((6,)),
            pltpu.VMEM((blocks * rows, lanes), f32),
            pltpu.VMEM((blocks * rows, lanes), f32),
            pltpu.VMEM((passes, PARTS, 2, part * rows, lanes), bf16),
            pltpu.VMEM((passes, PARTS, 2, part * rows, lanes), bf16),
            pltpu.VMEM((passes, PARTS, 2, lat_rows, lanes), bf16),
            pltpu.VMEM((passes, PARTS, 2, lat_rows, lanes), bf16),
            pltpu.VMEM((passes, PARTS, 2, 1, part * levels * rows), f32),
            pltpu.VMEM((passes, PARTS, 2, 1, part * levels * rows), f32),
            pltpu.VMEM((group * height, lanes), f32),
            pltpu.VMEM((group * height, lanes), f32),
            pltpu.VMEM((group * height, lanes), f32),
            pltpu.VMEM((group * height, lanes), f32),
            pltpu.VMEM((2, 2, 8, lanes), f32),
            pltpu.VMEM((2, group, 8, lanes), f32),
            pltpu.VMEM((2, n_lev, 8, lanes), f32),
            dma((passes, PARTS, 3, 2)),
            dma((passes, PARTS, 3, 2)),
            dma((2, group)),
            dma((2, group)),
            dma((2, group)),
            dma((2, group)),
            dma((2, n_lev)),
            dma((2, n_lev)),
        ],
        compiler_params=pltpu.CompilerParams(
            collective_id=0, has_side_effects=True, vmem_limit_bytes=56 * 1024 * 1024
        ),
        cost_estimate=pl.CostEstimate(flops=10**8, bytes_accessed=3 * 10**6, transcendentals=0),
        name="cg_step",
    )(
        direction,
        residual,
        ensemble,
        static_sd,
        obs_weight,
        obs_precision,
        jnp.swapaxes(send_tile, 3, 4),
        pair_count,
    )
    new_residual = residual - step * image
    return (
        solution + step * direction,
        new_residual,
        new_residual + ratio * direction,
    )


def solution(mesh):
    sizes = tuple(mesh.shape[axis] for axis in AXES)
    field = P(None, "lev", "lat", "lon")
    in_specs = (
        field,
        field,
        field,
        P(None, None, "lev", "lat", "lon"),
        field,
        P("lev", "lon", "lat", None, None),
        P("lev", "lon", "lat", None),
        P("lev", "lon", "lat", None, None, None, None),
        P("lev", "lon", "lat", None, None, None),
    )
    return jax.shard_map(
        functools.partial(body, sizes),
        mesh=mesh,
        in_specs=in_specs,
        out_specs=(field, field, field),
        check_vma=False,
    )
```

```python
import functools

import jax
import jax.numpy as jnp
from jax import lax
from jax.experimental import pallas as pl
from jax.experimental.pallas import tpu as pltpu
from jax.sharding import PartitionSpec as P

spread_lon = 0.075
spread_lat = 0.3
spread_lev = 0.075
ens_share = 0.75
static_part = 0.5
centre_share = 1.0 - 2.0 * (spread_lon + spread_lat + spread_lev)
PASSES = 4
PARTS = 2
AXES = ("lon", "lat", "lev")
MESH = pl.DeviceIdType.MESH
f32 = jnp.float32
bf16 = jnp.bfloat16


def each(count, step):
    if count <= 32:
        for k in range(count):
            step(k)
    else:
        lax.fori_loop(0, count, lambda k, carry: (step(k), carry)[1], 0)


def kernel(
    sizes,
    direction_hbm,
    residual_hbm,
    ensemble_hbm,
    static_sd_hbm,
    obs_weight_hbm,
    obs_precision_hbm,
    send_tile,
    pair_count,
    image_out,
    step_out,
    ratio_out,
    direction,
    residual,
    ensemble,
    static_sd,
    obs_weight,
    obs_precision,
    fetch_sem,
    field_a,
    field_b,
    lev_send,
    lev_recv,
    lat_send,
    lat_recv,
    lon_send,
    lon_recv,
    tiles_out,
    tiles_in,
    ret_out,
    ret_in,
    sum_send,
    sum_plane,
    sum_lev,
    sum_all,
    all_ssem,
    all_rsem,
    halo_ssem,
    halo_rsem,
    a2a_ssem,
    a2a_rsem,
    plane_ssem,
    plane_rsem,
    col_ssem,
    col_rsem,
):
    n_lon, n_lat, n_lev = sizes
    members, variables, levels, rows, lanes = ensemble.shape
    fields = direction.shape[0]
    blocks = fields * levels
    group = n_lon * n_lat
    slots = send_tile.shape[3]
    tiles = levels * rows
    scale_ens = (ens_share / members) ** 0.5
    at_lon, at_lat, at_lev = (lax.axis_index(a) for a in AXES)
    held = (direction, residual, ensemble, static_sd, obs_weight, obs_precision)
    origins = (
        direction_hbm,
        residual_hbm,
        ensemble_hbm,
        static_sd_hbm,
        obs_weight_hbm,
        obs_precision_hbm,
    )
    fetches = [
        pltpu.make_async_copy(src, dst, fetch_sem.at[i])
        for i, (src, dst) in enumerate(zip(origins, held))
    ]
    for fetch in fetches:
        fetch.start()
    me = at_lon * n_lat + at_lat

    def plane_id(k):
        peer = lax.rem(me + k, group)
        return peer, {"lon": peer // n_lat, "lat": lax.rem(peer, n_lat)}

    def lev_id(k):
        return {"lev": lax.rem(at_lev + k, n_lev)}

    barrier = pltpu.get_barrier_semaphore()

    def greet_plane(k):
        pl.semaphore_signal(barrier, inc=1, device_id=plane_id(k + 1)[1], device_id_type=MESH)

    def greet_lev(k):
        pl.semaphore_signal(barrier, inc=1, device_id=lev_id(k + 1), device_id_type=MESH)

    everyone = n_lev * group
    flat = everyone <= 32

    def any_id(q):
        return {**plane_id(q % group)[1], **lev_id(q // group)}

    if flat:
        for q in range(1, everyone):
            pl.semaphore_signal(barrier, inc=1, device_id=any_id(q), device_id_type=MESH)
    else:
        each(group - 1, greet_plane)
        each(n_lev - 1, greet_lev)

    buffers = {"lev": (lev_send, lev_recv), "lat": (lat_send, lat_recv), "lon": (lon_send, lon_recv)}
    places = {"lev": (at_lev, n_lev), "lat": (at_lat, n_lat), "lon": (at_lon, n_lon)}

    def halo_copy(p, h, axis, side):
        src, dst = buffers[axis]
        place, count = places[axis]
        number = AXES.index(axis)
        return pltpu.make_async_remote_copy(
            src_ref=src.at[p, h, side],
            dst_ref=dst.at[p, h, 1 - side],
            send_sem=halo_ssem.at[p, h, number, side],
            recv_sem=halo_rsem.at[p, h, number, 1 - side],
            device_id={axis: lax.rem(place + (count - 1 if side == 0 else 1), count)},
            device_id_type=MESH,
        )

    def if_there(axis, side, act):
        place, count = places[axis]
        if axis == "lon":
            act()
        else:
            pl.when(place > 0 if side == 0 else place < count - 1)(act)

    lane_of = lax.broadcasted_iota(jnp.int32, (1, rows, lanes), 2)
    row_of = lax.broadcasted_iota(jnp.int32, (1, rows, lanes), 1)
    west = jnp.where(lane_of > 0, spread_lon, 0.0)
    east = jnp.where(lane_of < lanes - 1, spread_lon, 0.0)
    south = jnp.where(row_of > 0, spread_lat, 0.0)
    north = jnp.where(row_of < rows - 1, spread_lat, 0.0)
    edge_row = lax.broadcasted_iota(jnp.int32, (8, lanes), 0)
    edge_lane = lax.broadcasted_iota(jnp.int32, (8, lanes), 1)
    edges = ((edge_row == 0) & (edge_lane == 0)) | ((edge_row == 1) & (edge_lane == lanes - 1))
    edges = edges.astype(bf16)
    part_fields = fields // PARTS
    part_blocks = part_fields * levels
    part_rows = part_blocks * rows
    lat_pad = lat_send.shape[3] - part_blocks

    def send_halos(p, h, src):
        start = h * part_rows
        x = src[start : start + part_rows, :]
        x4 = x.reshape(part_fields, levels, rows, lanes)
        for side, level in ((0, 0), (1, levels - 1)):
            lev_send[p, h, side] = x4[:, level].reshape(part_fields * rows, lanes).astype(bf16)
            if_there("lev", side, lambda side=side: halo_copy(p, h, "lev", side).start())
        packed = lax.dot_general(
            edges, x.astype(bf16), (((1,), (1,)), ((), ())), preferred_element_type=f32
        )
        for side, row in ((0, 0), (1, rows - 1)):
            edge = src[pl.ds(start + row, part_blocks, stride=rows), :]
            if lat_pad:
                edge = jnp.concatenate([edge, jnp.zeros((lat_pad, lanes), f32)], axis=0)
            lat_send[p, h, side] = edge.astype(bf16)
            if_there("lat", side, lambda side=side: halo_copy(p, h, "lat", side).start())
        for side in (0, 1):
            lon_send[p, h, side] = packed[side : side + 1]
            halo_copy(p, h, "lon", side).start()

    chunk = max(c for c in range(1, 10) if part_fields % c == 0)

    def local_part(h, src, dst):
        for first in range(0, part_fields, chunk):
            span = pl.ds(h * part_rows + first * levels * rows, chunk * levels * rows)
            x = src[span, :].reshape(chunk * levels, rows, lanes)
            y = x * centre_share
            y = y + west * pltpu.roll(x, 1, 2) + east * pltpu.roll(x, lanes - 1, 2)
            y = y + south * pltpu.roll(x, 1, 1) + north * pltpu.roll(x, rows - 1, 1)
            x4 = x.reshape(chunk, levels, rows, lanes)
            if levels > 1:
                none = jnp.zeros((chunk, 1, rows, lanes), f32)
                above = jnp.concatenate([x4[:, 1:], none], axis=1)
                below = jnp.concatenate([none, x4[:, :-1]], axis=1)
                y = y + spread_lev * (above + below).reshape(chunk * levels, rows, lanes)
            dst[span, :] = y.reshape(chunk * levels * rows, lanes)

    def add_halos(p, h, dst):
        start = h * part_rows
        for side in (0, 1):
            halo_copy(p, h, "lon", 1 - side).wait_recv()
        ends = jnp.concatenate(
            [lon_recv[p, h, 0], lon_recv[p, h, 1], jnp.zeros((6, part_rows), f32)], axis=0
        )
        spill = lax.dot_general(
            ends.astype(bf16), edges, (((0,), (0,)), ((), ())), preferred_element_type=f32
        )
        for side, row in ((0, 0), (1, rows - 1)):
            if_there("lat", side, lambda side=side: halo_copy(p, h, "lat", 1 - side).wait_recv())
            edge = lat_recv[p, h, side].astype(f32)[:part_blocks]
            at = pl.ds(start + row, part_blocks, stride=rows)
            dst[at, :] = dst[at, :] + spread_lat * edge
        for side in (0, 1):
            if_there("lev", side, lambda side=side: halo_copy(p, h, "lev", 1 - side).wait_recv())
        low = lev_recv[p, h, 0].astype(f32).reshape(part_fields, 1, rows, lanes) * spread_lev
        high = lev_recv[p, h, 1].astype(f32).reshape(part_fields, 1, rows, lanes) * spread_lev
        y = dst[start : start + part_rows, :] + spread_lon * spill
        y4 = y.reshape(part_fields, levels, rows, lanes)
        if levels == 1:
            y4 = y4 + low + high
        else:
            inner = [y4[:, 1:-1]] if levels > 2 else []
            y4 = jnp.concatenate([y4[:, :1] + low, *inner, y4[:, -1:] + high], axis=1)
        dst[start : start + part_rows, :] = y4.reshape(part_rows, lanes)

    def smooth(first_pass, meanwhile):
        src, dst = field_a, field_b
        for p in range(first_pass, first_pass + PASSES):
            for h in range(PARTS):
                if p == first_pass and h == 0:
                    meanwhile()
                local_part(h, src, dst)
                add_halos(p, h, dst)
                if p < first_pass + PASSES - 1:
                    send_halos(p + 1, h, dst)
            src, dst = dst, src
        return src

    for side in (0, 1):
        for axis in ("lat", "lev"):
            place, count = places[axis]

            def clear(axis=axis, side=side):
                ref = buffers[axis][1]
                for p in range(2 * PASSES):
                    for h in range(PARTS):
                        ref[p, h, side] = jnp.zeros(ref.shape[3:], ref.dtype)

            pl.when(place == 0 if side == 0 else place == count - 1)(clear)

    total = slots * group

    def slot_code(i):
        s, d = i // group, i % group
        tile = send_tile[0, 0, 0, s, d]
        return jnp.where(s < pair_count[0, 0, 0, d], tile, -1)

    def fill(dim, shape):
        where_at = lax.broadcasted_iota(jnp.int32, shape, dim)
        step = lambda i, codes: jnp.where(where_at == i, slot_code(i), codes)
        codes = jnp.zeros(shape, jnp.int32)
        if total <= 32:
            for i in range(total):
                codes = step(i, codes)
        else:
            codes = lax.fori_loop(0, total, step, codes)
        return (codes == lax.broadcasted_iota(jnp.int32, shape, 1 - dim)).astype(f32)

    pick = fill(0, (total, tiles)).astype(bf16)
    place_back = fill(1, (tiles, total))

    obs = obs_precision.shape[5]
    eye = (
        lax.broadcasted_iota(jnp.int32, (1, obs, obs), 1)
        == lax.broadcasted_iota(jnp.int32, (1, obs, obs), 2)
    ).astype(f32)
    fetches[0].wait()
    field_a[...] = direction[...].reshape(blocks * rows, lanes)
    pl.semaphore_wait(barrier, everyone - 1 if flat else group - 1 + n_lev - 1)
    for h in range(PARTS):
        send_halos(0, h, field_a)

    known = []

    def local_sums():
        for fetch in fetches[1:]:
            fetch.wait()
        for s in range(slots):
            row = obs_precision[0, 0, 0][:, s : s + 1, :]
            known.append(jnp.sum(row * eye, axis=2, keepdims=True))
        d_all = direction[...]
        r_all = residual[...]
        known.append(jnp.sum(d_all * d_all))
        known.append(jnp.sum(r_all * r_all))

    smoothed = smooth(0, local_sums)
    precision, direction_norm, residual_norm = known[:slots], known[slots], known[slots + 1]

    sm4 = smoothed[...].reshape(fields, levels, rows, lanes)
    ens_part = jnp.zeros((variables, levels, rows, lanes), f32)
    for k in range(members):
        ens_part = ens_part + ensemble[k].astype(f32) * sm4[k][None]
    increment = scale_ens * ens_part + static_part * static_sd[...] * sm4[members:]
    increment = increment.astype(bf16).reshape(variables, tiles, lanes)
    table = jnp.concatenate([increment[v] for v in range(variables)], axis=1)
    outgoing = jnp.dot(pick, table, preferred_element_type=f32)
    height = slots * variables
    for s in range(slots):
        for v in range(variables):
            part = outgoing[s * group : (s + 1) * group, v * lanes : (v + 1) * lanes]
            tiles_out[pl.ds(s * variables + v, group, stride=height), :] = part

    def block_of(ref, g):
        return ref.at[pl.ds(pl.multiple_of(g * height, height), height), :]

    def exchange(turn, src, dst):
        def copy(k):
            peer, device = plane_id(k + 1)
            return pltpu.make_async_remote_copy(
                src_ref=block_of(src, peer),
                dst_ref=block_of(dst, me),
                send_sem=a2a_ssem.at[turn, k],
                recv_sem=a2a_rsem.at[turn, k],
                device_id=device,
                device_id_type=MESH,
            )

        return copy

    def own_block(src, dst):
        block_of(dst, me)[...] = block_of(src, me)[...]

    there = exchange(0, tiles_out, tiles_in)
    each(group - 1, lambda k: there(k).start())
    own_block(tiles_out, tiles_in)
    each(group - 1, lambda k: there(k).wait_recv())

    arrived = tiles_in[...].reshape(group, height, lanes)
    fit = jnp.zeros((1, 1), f32)
    for s in range(slots):
        weights = [
            obs_weight[0, 0, 0, :, s, :, v * lanes : (v + 1) * lanes].astype(f32)
            for v in range(variables)
        ]
        product = jnp.zeros((group, obs, lanes), f32)
        for v in range(variables):
            at = s * variables + v
            product = product + weights[v] * arrived[:, at : at + 1, :]
        predicted = jnp.sum(product, axis=2, keepdims=True)
        weighted = (precision[s] * predicted).astype(bf16).astype(f32)
        fit = fit + jnp.sum(jnp.sum(predicted * weighted, axis=0), axis=0, keepdims=True)
        for v in range(variables):
            ret = jnp.sum(weights[v] * weighted, axis=1, keepdims=True)
            ret_out[pl.ds(s * variables + v, group, stride=height), :] = ret.reshape(group, lanes)

    back_again = exchange(1, ret_out, ret_in)
    each(group - 1, lambda k: back_again(k).start())
    own_block(ret_out, ret_in)

    def sum_copies(turn):
        def plane(k):
            return pltpu.make_async_remote_copy(
                src_ref=sum_send.at[turn, 0],
                dst_ref=sum_plane.at[turn, k + 1],
                send_sem=plane_ssem.at[turn, k],
                recv_sem=plane_rsem.at[turn, k],
                device_id=plane_id(k + 1)[1],
                device_id_type=MESH,
            )

        def column(k):
            return pltpu.make_async_remote_copy(
                src_ref=sum_send.at[turn, 1],
                dst_ref=sum_lev.at[turn, k + 1],
                send_sem=col_ssem.at[turn, k],
                recv_sem=col_rsem.at[turn, k],
                device_id=lev_id(k + 1),
                device_id_type=MESH,
            )

        return plane, column

    def sum_begin(turn, values):
        plane, column = sum_copies(turn)
        sum_send[turn, 0] = values
        sum_plane[turn, 0] = values
        each(group - 1, lambda k: plane(k).start())

    def sum_middle(turn):
        plane, column = sum_copies(turn)
        each(group - 1, lambda k: plane(k).wait_recv())
        values = jnp.sum(sum_plane[turn], axis=0)
        sum_send[turn, 1] = values
        sum_lev[turn, 0] = values
        each(n_lev - 1, lambda k: column(k).start())

    def sum_end(turn):
        plane, column = sum_copies(turn)
        each(n_lev - 1, lambda k: column(k).wait_recv())
        return jnp.sum(sum_lev[turn], axis=0)

    row8 = lax.broadcasted_iota(jnp.int32, (8, lanes), 0)
    mine = jnp.where(row8 == 0, residual_norm, jnp.where(row8 == 1, direction_norm, 0.0))
    sum_begin(0, mine + jnp.where(row8 == 2, fit, 0.0))

    each(group - 1, lambda k: back_again(k).wait_recv())
    came = jnp.concatenate(
        [
            jnp.concatenate(
                [
                    ret_in[pl.ds(s * variables + v, group, stride=height), :]
                    for v in range(variables)
                ],
                axis=1,
            )
            for s in range(slots)
        ],
        axis=0,
    )
    adjoint = jnp.dot(
        place_back, came, precision=lax.Precision.HIGHEST, preferred_element_type=f32
    )
    adjoint = jnp.stack(
        [
            adjoint[:, v * lanes : (v + 1) * lanes].reshape(levels, rows, lanes)
            for v in range(variables)
        ]
    )
    scaled = scale_ens * adjoint
    deep = levels * rows
    def tell(k):
        if (k + 1) % part_fields == 0:
            send_halos(PASSES, (k + 1) // part_fields - 1, field_a)

    for k in range(members):
        value = jnp.sum(ensemble[k].astype(f32) * scaled, axis=0)
        field_a[k * deep : (k + 1) * deep, :] = value.reshape(deep, lanes)
        tell(k)
    still = static_part * static_sd[...] * adjoint
    field_a[members * deep :, :] = still.reshape(variables * deep, lanes)
    send_halos(PASSES, PARTS - 1, field_a)

    smooth_back = smooth(PASSES, lambda: sum_middle(0))

    totals = sum_end(0)
    start_norm = totals[0:1]
    step = start_norm / (totals[1:2] + totals[2:3])
    image = direction[...] + smooth_back[...].reshape(fields, levels, rows, lanes)
    image_out[...] = image
    left = residual[...] - step * image
    next_norm = jnp.sum(left * left)
    spread = jnp.full((8, lanes), next_norm, f32)

    def to_any(q):
        return pltpu.make_async_remote_copy(
            src_ref=sum_all.at[0],
            dst_ref=sum_all.at[q],
            send_sem=all_ssem.at[q],
            recv_sem=all_rsem.at[q],
            device_id=any_id(q),
            device_id_type=MESH,
        )

    if flat:
        sum_all[0] = spread
        for q in range(1, everyone):
            to_any(q).start()
        for q in range(1, everyone):
            to_any(q).wait_recv()
        totals = jnp.sum(sum_all[...], axis=0)
        for q in range(1, everyone):
            to_any(q).wait_send()
    else:
        sum_begin(1, spread)
        sum_middle(1)
        totals = sum_end(1)
    ratio = totals / (start_norm + 1e-6)
    step_out[...] = jnp.broadcast_to(step, (8, lanes))
    ratio_out[...] = ratio

    for p in range(2 * PASSES):
        for h in range(PARTS):
            for axis in AXES:
                for side in (0, 1):
                    if_there(axis, side, lambda: halo_copy(p, h, axis, side).wait_send())
    for copy in (there, back_again):
        each(group - 1, lambda k: copy(k).wait_send())
    for turn in (0,) if flat else (0, 1):
        plane, column = sum_copies(turn)
        each(group - 1, lambda k: plane(k).wait_send())
        each(n_lev - 1, lambda k: column(k).wait_send())


def body(
    sizes,
    solution,
    residual,
    direction,
    ensemble,
    static_sd,
    send_tile,
    pair_count,
    obs_weight,
    obs_precision,
):
    n_lon, n_lat, n_lev = sizes
    members, variables, levels, rows, lanes = ensemble.shape
    fields = direction.shape[0]
    blocks = fields * levels
    group = n_lon * n_lat
    slots = send_tile.shape[4]
    height = slots * variables
    passes = 2 * PASSES
    part = fields // PARTS
    lat_rows = -(-(part * levels) // 16) * 16
    vmem = pl.BlockSpec(memory_space=pltpu.VMEM)
    smem = pl.BlockSpec(memory_space=pltpu.SMEM)
    dma = pltpu.SemaphoreType.DMA
    image, step, ratio = pl.pallas_call(
        functools.partial(kernel, sizes),
        out_shape=[
            jax.ShapeDtypeStruct(direction.shape, f32),
            jax.ShapeDtypeStruct((8, lanes), f32),
            jax.ShapeDtypeStruct((8, lanes), f32),
        ],
        in_specs=[pl.BlockSpec(memory_space=pl.ANY)] * 6 + [smem] * 2,
        out_specs=[vmem] * 3,
        scratch_shapes=[
            pltpu.VMEM(direction.shape, f32),
            pltpu.VMEM(residual.shape, f32),
            pltpu.VMEM(ensemble.shape, bf16),
            pltpu.VMEM(static_sd.shape, f32),
            pltpu.VMEM(obs_weight.shape, bf16),
            pltpu.VMEM(obs_precision.shape, f32),
            dma((6,)),
            pltpu.VMEM((blocks * rows, lanes), f32),
            pltpu.VMEM((blocks * rows, lanes), f32),
            pltpu.VMEM((passes, PARTS, 2, part * rows, lanes), bf16),
            pltpu.VMEM((passes, PARTS, 2, part * rows, lanes), bf16),
            pltpu.VMEM((passes, PARTS, 2, lat_rows, lanes), bf16),
            pltpu.VMEM((passes, PARTS, 2, lat_rows, lanes), bf16),
            pltpu.VMEM((passes, PARTS, 2, 1, part * levels * rows), f32),
            pltpu.VMEM((passes, PARTS, 2, 1, part * levels * rows), f32),
            pltpu.VMEM((group * height, lanes), f32),
            pltpu.VMEM((group * height, lanes), f32),
            pltpu.VMEM((group * height, lanes), f32),
            pltpu.VMEM((group * height, lanes), f32),
            pltpu.VMEM((2, 2, 8, lanes), f32),
            pltpu.VMEM((2, group, 8, lanes), f32),
            pltpu.VMEM((2, n_lev, 8, lanes), f32),
            pltpu.VMEM((min(32, n_lev * group), 8, lanes), f32),
            dma((min(32, n_lev * group),)),
            dma((min(32, n_lev * group),)),
            dma((passes, PARTS, 3, 2)),
            dma((passes, PARTS, 3, 2)),
            dma((2, group)),
            dma((2, group)),
            dma((2, group)),
            dma((2, group)),
            dma((2, n_lev)),
            dma((2, n_lev)),
        ],
        compiler_params=pltpu.CompilerParams(
            collective_id=0, has_side_effects=True, vmem_limit_bytes=56 * 1024 * 1024
        ),
        cost_estimate=pl.CostEstimate(flops=10**8, bytes_accessed=3 * 10**6, transcendentals=0),
        name="cg_step",
    )(
        direction,
        residual,
        ensemble,
        static_sd,
        obs_weight,
        obs_precision,
        jnp.swapaxes(send_tile, 3, 4),
        pair_count,
    )
    new_residual = residual - step * image
    return (
        solution + step * direction,
        new_residual,
        new_residual + ratio * direction,
    )


def solution(mesh):
    sizes = tuple(mesh.shape[axis] for axis in AXES)
    field = P(None, "lev", "lat", "lon")
    in_specs = (
        field,
        field,
        field,
        P(None, None, "lev", "lat", "lon"),
        field,
        P("lev", "lon", "lat", None, None),
        P("lev", "lon", "lat", None),
        P("lev", "lon", "lat", None, None, None, None),
        P("lev", "lon", "lat", None, None, None),
    )
    return jax.shard_map(
        functools.partial(body, sizes),
        mesh=mesh,
        in_specs=in_specs,
        out_specs=(field, field, field),
        check_vma=False,
    )
```
